32 devices in a mesh: dp: 2 (over x), ctx: 4 (over y, core), tp: 4 (over z).
Axes of the slice: x: 2, y: 2, z: 4, core: 2. Of those that a mesh axis runs over, the one named last changes fastest.
Arguments:
- tokens: bfloat16 [8, 2048, 768], P('dp', 'ctx'), may hold values from -6 to 6
- cotangent: bfloat16 [8, 2048, 768], P('dp', 'ctx'), may hold values from -6 to 6
- routes: int32 [8, 2048, 1], P('dp', 'ctx'), may hold values from 0 to 1; in each aligned block of 512 rows (0 to 511, 512 to 1023, ..., all dimensions but the last counted through in order) at most 384 rows name the same one
- qkv_weight: float32 [768, 3, 768], P('dp', None, 'tp'), may hold values from -0.21875 to 0.21875
- out_weight: float32 [768, 768], P('dp', 'tp'), may hold values from -3.5 to 3.5
- router_weight: float32 [768, 2], P('dp'), may hold values from -0.15625 to 0.15625
- bias_table: float32 [32, 12], P('dp', 'tp'), may hold values from -4 to 4
- norm_gains: float32 [768, 2], P('dp'), may hold values from 0.5 to 1.5
- expert_in: float32 [2, 768, 3072], P('dp', None, 'tp'), may hold values from -0.21875 to 0.21875
- expert_down: float32 [2, 3072, 768], P('dp', 'tp'), may hold values from -0.21875 to 0.21875
- qkv_first: float32 [768, 3, 768], P('dp', None, 'tp')
- qkv_second: float32 [768, 3, 768], P('dp', None, 'tp')
- out_first: float32 [768, 768], P('dp', 'tp')
- out_second: float32 [768, 768], P('dp', 'tp')
- router_first: float32 [768, 2], P('dp')
- router_second: float32 [768, 2], P('dp')
- table_first: float32 [32, 12], P('dp', 'tp')
- table_second: float32 [32, 12], P('dp', 'tp')
- gains_first: float32 [768, 2], P('dp')
- gains_second: float32 [768, 2], P('dp')
- in_first: float32 [2, 768, 3072], P('dp', None, 'tp')
- in_second: float32 [2, 768, 3072], P('dp', None, 'tp')
- down_first: float32 [2, 3072, 768], P('dp', 'tp')
- down_second: float32 [2, 3072, 768], P('dp', 'tp')
Outputs:
- mixed: bfloat16 [8, 2048, 768], P('dp', 'ctx')
- tokens_grad: float32 [8, 2048, 768], P('dp', 'ctx')
- query_key_value_first_moment_new: float32 [768, 3, 768], P('dp', None, 'tp')
- qkv_second_new: float32 [768, 3, 768], P('dp', None, 'tp')
- qkv_weight_new: float32 [768, 3, 768], P('dp', None, 'tp')
- out_first_new: float32 [768, 768], P('dp', 'tp')
- out_second_new: float32 [768, 768], P('dp', 'tp')
- out_weight_new: float32 [768, 768], P('dp', 'tp')
- router_first_new: float32 [768, 2], P('dp')
- router_second_new: float32 [768, 2], P('dp')
- router_weight_new: float32 [768, 2], P('dp')
- table_first_new: float32 [32, 12], P('dp', 'tp')
- table_second_new: float32 [32, 12], P('dp', 'tp')
- table_weight_new: float32 [32, 12], P('dp', 'tp')
- gains_first_new: float32 [768, 2], P('dp')
- gains_second_new: float32 [768, 2], P('dp')
- gains_weight_new: float32 [768, 2], P('dp')
- in_first_new: float32 [2, 768, 3072], P('dp', None, 'tp')
- in_second_new: float32 [2, 768, 3072], P('dp', None, 'tp')
- in_weight_new: float32 [2, 768, 3072], P('dp', None, 'tp')
- down_first_new: float32 [2, 3072, 768], P('dp', 'tp')
- down_second_new: float32 [2, 3072, 768], P('dp', 'tp')
- down_weight_new: float32 [2, 3072, 768], P('dp', 'tp')
The draws below stay inside these ranges and needn't reach their ends.
Inputs may be any that keep to these rules, and one draw needn't show every extreme that they name: `routes`: in each block of 512 positions of a sequence (one device's tokens of it) no expert is named by more than 384 tokens, and some block reaches 384.
All inputs are finite; a program needn't handle non-finite values.
Results may differ from the reference program's by a relative error of at most 0.017.
The reference program's roundings to bfloat16 on the way count: a program that leaves them out, or rounds other values in their place, can miss the bound.
Values may be sent and summed in bfloat16 or wider, within the bound.
A program may use at most 320 MiB of HBM per device.

```python
import math
import jax
import jax.numpy as jnp
import numpy as np
from jax import lax

D = 768
HEADS = 12
HEAD_DIM = 64
FF = 3072
BUCKETS = 32
LENGTH = 2048
STEP = 10
EXPERTS = 2
BLK = 512
SEQUENCES = 8
TOKENS = 16384
MOST = 384
N_CTX = 4


def momentum_draw(key, array_shape, grad_size):
    return jax.random.normal(key, array_shape, jnp.float32) * (grad_size * 0.1 / 0.9)


def variance_draw(key, array_shape, grad_size):
    spread = jnp.exp(jax.random.uniform(key, array_shape, jnp.float32, math.log(0.5), math.log(8.0)))
    return spread * (grad_size * grad_size * 0.001 / 0.999)


def draw_qkv_first(key, part):
    key = jax.random.fold_in(key, 11)
    return momentum_draw(key, (D, 3, D), 1.3 * math.sqrt(TOKENS))


def draw_qkv_second(key, part):
    key = jax.random.fold_in(key, 12)
    return variance_draw(key, (D, 3, D), 1.3 * math.sqrt(TOKENS))


def draw_out_first(key, part):
    key = jax.random.fold_in(key, 13)
    return momentum_draw(key, (D, D), 1.3 * math.sqrt(8.0 * TOKENS / LENGTH))


def draw_out_second(key, part):
    key = jax.random.fold_in(key, 14)
    return variance_draw(key, (D, D), 1.3 * math.sqrt(8.0 * TOKENS / LENGTH))


def draw_router_first(key, part):
    key = jax.random.fold_in(key, 15)
    return momentum_draw(key, (D, EXPERTS), 0.8 * math.sqrt(TOKENS * D / EXPERTS))


def draw_router_second(key, part):
    key = jax.random.fold_in(key, 16)
    return variance_draw(key, (D, EXPERTS), 0.8 * math.sqrt(TOKENS * D / EXPERTS))


def draw_table_first(key, part):
    key = jax.random.fold_in(key, 17)
    return momentum_draw(key, (BUCKETS, HEADS), 1.5 * math.sqrt(TOKENS))


def draw_table_second(key, part):
    key = jax.random.fold_in(key, 18)
    return variance_draw(key, (BUCKETS, HEADS), 1.5 * math.sqrt(TOKENS))


def draw_gains_first(key, part):
    key = jax.random.fold_in(key, 19)
    return momentum_draw(key, (D, 2), 1.5 * math.sqrt(TOKENS))


def draw_gains_second(key, part):
    key = jax.random.fold_in(key, 20)
    return variance_draw(key, (D, 2), 1.5 * math.sqrt(TOKENS))


def draw_in_first(key, part):
    key = jax.random.fold_in(key, 21)
    return momentum_draw(key, (EXPERTS, D, FF), 0.35 * math.sqrt(TOKENS / EXPERTS))


def draw_in_second(key, part):
    key = jax.random.fold_in(key, 22)
    return variance_draw(key, (EXPERTS, D, FF), 0.35 * math.sqrt(TOKENS / EXPERTS))


def draw_down_first(key, part):
    key = jax.random.fold_in(key, 23)
    return momentum_draw(key, (EXPERTS, FF, D), 0.65 * math.sqrt(TOKENS / EXPERTS) / EXPERTS)


def draw_down_second(key, part):
    key = jax.random.fold_in(key, 24)
    return variance_draw(key, (EXPERTS, FF, D), 0.65 * math.sqrt(TOKENS / EXPERTS) / EXPERTS)


def shard_levels(key, dims, split, low, high):
    def one(axis_at, shards_of):
        heights = jax.random.uniform(jax.random.fold_in(jax.random.fold_in(key, 6), axis_at), (shards_of,), jnp.float32, low / len(split), high / len(split))
        return jnp.repeat(jnp.exp(heights), dims[axis_at] // shards_of).reshape((-1,) + (1,) * (len(dims) - axis_at - 1))

    factor_of = one(*split[0])
    for cut in split[1:]:
        factor_of = factor_of * one(*cut)
    return factor_of


def routed_block(rng, own, number, rows, amount, top, reach, slope):
    sequence = jax.random.permutation(rng, amount)
    crowded, ordinary = shares(amount, rows * top, reach, slope, True), shares(amount, rows * top, reach, slope, False)
    places = jnp.arange(amount)

    def named(lengths, rotation):
        used = int((lengths > 0).sum())
        fixed = max(1, used // 4)
        shifted = fixed + (places - fixed + rotation * (used - fixed)) % max(1, amount - fixed)
        return jnp.zeros((amount,), jnp.int32).at[sequence[jnp.where(places < fixed, places, shifted)]].set(jnp.asarray(lengths, jnp.int32))

    lengths = jnp.where(number % 4 == 0, named(crowded, number // 4), named(ordinary, number - number // 4 - 1))
    mixed = jax.random.permutation(jax.random.fold_in(own, 3), amount)
    source_of, receiver = mixed[0:amount // 2 * 2:2], mixed[1:amount // 2 * 2:2]
    slack = jnp.minimum(lengths[source_of] - 1, reach - lengths[receiver]) // 2
    slack = jnp.where((source_of == sequence[0]) | (receiver == sequence[0]) | (lengths[receiver] == 0), 0, jnp.maximum(slack, 0))
    shifted = jax.random.randint(jax.random.fold_in(own, 4), (amount // 2,), 0, 1 << 20) % (slack + 1)
    lengths = lengths.at[source_of].add(-shifted).at[receiver].add(shifted)
    items = jnp.searchsorted(jnp.cumsum(lengths), jnp.arange(rows * top), side="right").astype(jnp.int32)
    table = items.reshape(top, rows).T
    table = table[jax.random.permutation(jax.random.fold_in(own, 1), rows)]
    rotation = jax.random.randint(jax.random.fold_in(own, 2), (rows, 1), 0, top)
    return jnp.take_along_axis(table, (jnp.arange(top)[None, :] + rotation) % top, axis=1)


def shares(count, total, limit, lean, full):
    loads = [(1 << 20) // math.isqrt(standing ** lean) + 1 for standing in range(1, count + 1)]
    largest = limit if full else min(limit, max(-(-total // count), total * loads[0] // sum(loads)))
    least = 1 if total - largest >= count - 1 else 0
    holding, surplus = [largest] + [least] * (count - 1), total - largest - least * (count - 1)
    while surplus > 0:
        free = [i for i in range(1, count) if holding[i] < largest] or [i for i in range(1, count) if holding[i] < limit]
        whole, budget = sum([loads[i] for i in free]), surplus
        for i in free:
            more = min(limit - holding[i], max(1, budget * loads[i] // whole), surplus)
            holding[i] = holding[i] + more
            surplus = surplus - more
    return np.array(holding)


def scatter_about(own_key, extent, scale, reach, cuts=(), kind=jnp.bfloat16):
    drawn = scale * jax.random.normal(own_key, extent, jnp.float32)
    if cuts:
        drawn = drawn * shard_levels(own_key, extent, cuts, -0.22, 0.18)
    return jnp.clip(drawn, -reach, reach).astype(kind)


def setup_inputs(seed: int = 0) -> dict:
    arg_keys = jax.random.split(jax.random.key(seed), 25)
    tokens = scatter_about(arg_keys[0], (SEQUENCES, LENGTH, D), 1.0, 6.0, ((0, 2), (1, 4)))
    cotangent = scatter_about(arg_keys[1], (SEQUENCES, LENGTH, D), 1.0, 6.0, ((0, 2), (1, 4)))
    routes_keys = jax.random.split(jax.random.fold_in(arg_keys[2], 1), SEQUENCES * LENGTH // BLK)
    routes_turns = jax.random.permutation(jax.random.fold_in(arg_keys[2], 3), SEQUENCES * LENGTH // BLK)
    routes = jax.vmap(lambda own, number: routed_block(jax.random.fold_in(arg_keys[2], 2), own, number, BLK, EXPERTS, 1, MOST, 1))(routes_keys, routes_turns).reshape((SEQUENCES, LENGTH, 1))
    qkv_weight = scatter_about(arg_keys[3], (D, 3, D), D ** -0.5, 0.21875, ((0, 2), (2, 4)), jnp.float32)
    out_weight = scatter_about(arg_keys[4], (D, D), (max(1, 8 * D // LENGTH)) ** -0.5, 3.5, ((0, 2), (1, 4)), jnp.float32)
    router_weight = scatter_about(arg_keys[5], (D, EXPERTS), (2 * D) ** -0.5, 0.15625, ((0, 2),), jnp.float32)
    bias_table = scatter_about(arg_keys[6], (BUCKETS, HEADS), 1.0, 4.0, ((0, 2), (1, 4)), jnp.float32)
    norm_gains = jnp.clip(1.0 + 0.1 * jax.random.normal(arg_keys[7], (D, 2), jnp.float32), 0.5, 1.5)
    expert_in = scatter_about(arg_keys[8], (EXPERTS, D, FF), D ** -0.5, 0.21875, ((0, 2), (2, 4)), jnp.float32)
    expert_down = scatter_about(arg_keys[9], (EXPERTS, FF, D), (max(1, FF // (EXPERTS * EXPERTS))) ** -0.5, 0.21875, ((0, 2), (1, 4)), jnp.float32)
    qkv_first = draw_qkv_first(jax.random.fold_in(arg_keys[24], 71), 0)
    qkv_second = draw_qkv_second(jax.random.fold_in(arg_keys[24], 71), 0)
    out_first = draw_out_first(jax.random.fold_in(arg_keys[24], 71), 0)
    out_second = draw_out_second(jax.random.fold_in(arg_keys[24], 71), 0)
    router_first = draw_router_first(jax.random.fold_in(arg_keys[24], 71), 0)
    router_second = draw_router_second(jax.random.fold_in(arg_keys[24], 71), 0)
    table_first = draw_table_first(jax.random.fold_in(arg_keys[24], 71), 0)
    table_second = draw_table_second(jax.random.fold_in(arg_keys[24], 71), 0)
    gains_first = draw_gains_first(jax.random.fold_in(arg_keys[24], 71), 0)
    gains_second = draw_gains_second(jax.random.fold_in(arg_keys[24], 71), 0)
    in_first = draw_in_first(jax.random.fold_in(arg_keys[24], 71), 0)
    in_second = draw_in_second(jax.random.fold_in(arg_keys[24], 71), 0)
    down_first = draw_down_first(jax.random.fold_in(arg_keys[24], 71), 0)
    down_second = draw_down_second(jax.random.fold_in(arg_keys[24], 71), 0)
    return {"tokens": tokens, "cotangent": cotangent, "routes": routes, "qkv_weight": qkv_weight, "out_weight": out_weight, "router_weight": router_weight, "bias_table": bias_table, "norm_gains": norm_gains, "expert_in": expert_in, "expert_down": expert_down, "qkv_first": qkv_first, "qkv_second": qkv_second, "out_first": out_first, "out_second": out_second, "router_first": router_first, "router_second": router_second, "table_first": table_first, "table_second": table_second, "gains_first": gains_first, "gains_second": gains_second, "in_first": in_first, "in_second": in_second, "down_first": down_first, "down_second": down_second}


@jax.custom_vjp
def low(v):
    return lax.optimization_barrier(v.astype(jnp.bfloat16)).astype(jnp.float32)

@jax.custom_vjp
def low_back(v):
    return v

def low_keep(v):
    return (low(v), None)

def low_pass(kept, grad):
    return (grad,)

def back_keep(v):
    return (v, None)

def back_low(kept, grad):
    return (low(grad),)
low.defvjp(low_keep, low_pass)
low_back.defvjp(back_keep, back_low)
thresholds = (12, 16, 23, 32, 46, 64, 91)
beta_one = 0.9
beta_two = 0.999
epsilon = 1e-08
decay = 0.01
highest = lax.Precision.HIGHEST

def bucket_of(query_pos, key_pos):
    offset = key_pos[None, :] - query_pos[:, None]
    distance = jnp.abs(offset)
    bucket = jnp.minimum(distance, 8)
    for border in thresholds:
        bucket = bucket + (distance >= border).astype(jnp.int32)
    return bucket + 16 * (offset > 0).astype(jnp.int32)

def rms_norm(values, gain_vector_row):
    return values * lax.rsqrt(lax.optimization_barrier(jnp.mean(values * values, axis=-1, keepdims=True)) + 1e-06) * gain_vector_row

def slot_of(routes_seq):
    grouped = routes_seq.reshape(N_CTX, BLK)
    onehot = (grouped[:, :, None] == jnp.arange(EXPERTS, dtype=jnp.int32)[None, None, :]).astype(jnp.int32)
    before = jnp.cumsum(onehot, axis=1) - onehot
    return lax.optimization_barrier(jnp.sum(before * onehot, axis=-1)).reshape(LENGTH).astype(jnp.int32)

def block_forward(params, inputs, routes_seq, buckets):
    w_qkv, w_out, w_router, bias_table_weight, w_gains, w_in, w_down = [low(weight) for weight in params]
    normed_one = low(rms_norm(inputs, w_gains[:, 0]))
    projected = jnp.einsum('rd,dtc->rtc', normed_one, w_qkv, precision=highest)
    projected = low(low_back(projected))
    queries = projected[:, 0].reshape(LENGTH, HEADS, HEAD_DIM)
    keys = projected[:, 1].reshape(LENGTH, HEADS, HEAD_DIM)
    values = projected[:, 2].reshape(LENGTH, HEADS, HEAD_DIM)
    relative_position_bias = jnp.transpose(bias_table_weight[buckets], (2, 0, 1))
    scores = jnp.einsum('qhd,khd->hqk', queries, keys, precision=highest) * HEAD_DIM ** (-0.5) + relative_position_bias
    scores = low_back(scores)
    attend = jax.nn.softmax(scores, axis=-1)
    heads_out = jnp.einsum('hqk,khd->qhd', low(attend), values, precision=highest).reshape(LENGTH, D)
    heads_out = low(low_back(heads_out))
    attention = low_back(jnp.dot(heads_out, w_out.T, precision=highest))
    hidden = inputs + attention
    normed_two = low(rms_norm(hidden, w_gains[:, 1]))
    logits = low_back(jnp.dot(normed_two, w_router, precision=highest))
    router_probs = jax.nn.softmax(logits, axis=-1)
    route_mask = routes_seq[:, None] == jnp.arange(EXPERTS, dtype=jnp.int32)[None, :]
    gate_value = lax.optimization_barrier(jnp.sum(jnp.where(route_mask, router_probs, 0.0), axis=-1))
    slot_index = slot_of(routes_seq)
    block_ids = (jnp.arange(LENGTH, dtype=jnp.int32) // BLK).astype(jnp.int32)
    buffer = jnp.zeros((N_CTX, EXPERTS, MOST, D), jnp.float32).at[block_ids, routes_seq, slot_index].set(normed_two)
    pre_act = low_back(jnp.einsum('cemd,edf->cemf', buffer, w_in, precision=highest))
    activated = low(jax.nn.gelu(pre_act, approximate=True))
    returned = jnp.einsum('cemf,efd->cemd', activated, w_down, precision=highest)
    returned = low(low_back(returned))
    expert_rows = returned[block_ids, routes_seq, slot_index]
    return hidden + gate_value[:, None] * expert_rows

def adamw(weight, gradient, moment_one, moment_two, step_rate):
    first_new = beta_one * moment_one + (1.0 - beta_one) * gradient
    second_new = beta_two * moment_two + (1.0 - beta_two) * gradient * gradient
    corrected_first = first_new / (1.0 - beta_one ** STEP)
    corrected_second = second_new / (1.0 - beta_two ** STEP)
    weight_new = weight - step_rate * (corrected_first / (jnp.sqrt(corrected_second) + epsilon) + decay * weight)
    return (first_new, second_new, weight_new)

def add_up(running, update):
    return running + update

def reference(tokens, cotangent, routes, qkv_weight, out_weight, router_weight, bias_table, norm_gains, expert_in, expert_down, qkv_first, qkv_second, out_first, out_second, router_first, router_second, table_first, table_second, gains_first, gains_second, in_first, in_second, down_first, down_second):
    params = (qkv_weight, out_weight, router_weight, bias_table, norm_gains, expert_in, expert_down)
    positions = jnp.arange(LENGTH, dtype=jnp.int32)
    buckets = bucket_of(positions, positions)

    def one_sequence(totals, inputs):
        seq_tokens, seq_cot, seq_routes = inputs

        def forward(params_in, tokens_in):
            return block_forward(params_in, tokens_in, seq_routes[:, 0], buckets)
        output, pullback = jax.vjp(forward, params, seq_tokens.astype(jnp.float32))
        param_grads, token_grads = pullback(seq_cot.astype(jnp.float32))
        totals = jax.tree.map(add_up, totals, param_grads)
        return (totals, (output.astype(jnp.bfloat16), token_grads))
    starting = tuple((jnp.zeros(weight.shape, jnp.float32) for weight in params))
    totals, (mixed, tokens_grad) = lax.scan(one_sequence, starting, (tokens, cotangent, routes))
    rates = (2.0 * D ** (-0.5), 2.0 * max(1, 8 * D // LENGTH) ** (-0.5), 2.0 * (2 * D) ** (-0.5), 2.0, 0.25, 2.0 * D ** (-0.5), 2.0 * max(1, FF // (EXPERTS * EXPERTS)) ** (-0.5))
    qkv_new = adamw(qkv_weight, totals[0], qkv_first, qkv_second, rates[0])
    out_new = adamw(out_weight, totals[1], out_first, out_second, rates[1])
    router_new = adamw(router_weight, totals[2], router_first, router_second, rates[2])
    table_new = adamw(bias_table, totals[3], table_first, table_second, rates[3])
    gains_new = adamw(norm_gains, totals[4], gains_first, gains_second, rates[4])
    in_new = adamw(expert_in, totals[5], in_first, in_second, rates[5])
    down_new = adamw(expert_down, totals[6], down_first, down_second, rates[6])
    return (mixed, tokens_grad, qkv_new[0], qkv_new[1], qkv_new[2], out_new[0], out_new[1], out_new[2], router_new[0], router_new[1], router_new[2], table_new[0], table_new[1], table_new[2], gains_new[0], gains_new[1], gains_new[2], in_new[0], in_new[1], in_new[2], down_new[0], down_new[1], down_new[2])
```

```python
import jax
import jax.numpy as jnp
from jax import lax
from jax.experimental import pallas as pl
from jax.experimental.pallas import tpu as pltpu
from jax.sharding import PartitionSpec as P

D = 768
HEAD_DIM = 64
FF = 3072
LENGTH = 2048
STEP = 10
TILE = 256
BAND = 5


thresholds = (12, 16, 23, 32, 46, 64, 91)
beta_one = 0.9
beta_two = 0.999
epsilon = 1e-08
decay = 0.01


def bucket_of(query_pos, key_pos):
    offset = key_pos[:, None] - query_pos[None, :]
    distance = jnp.abs(offset)
    bucket = jnp.minimum(distance, 8)
    for border in thresholds:
        bucket = bucket + (distance >= border).astype(jnp.int32)
    return bucket + 16 * (offset > 0).astype(jnp.int32)


def rms_norm(values, gain_vector_row):
    return (
        values
        * lax.rsqrt(jnp.mean(values * values, axis=-1, keepdims=True) + 1e-06)
        * gain_vector_row
    )


def adamw(weight, gradient, moment_one, moment_two, step_rate):
    first_new = beta_one * moment_one + (1.0 - beta_one) * gradient
    second_new = beta_two * moment_two + (1.0 - beta_two) * gradient * gradient
    corrected_first = first_new / (1.0 - beta_one**STEP)
    corrected_second = second_new / (1.0 - beta_two**STEP)
    weight_new = weight - step_rate * (
        corrected_first / (jnp.sqrt(corrected_second) + epsilon) + decay * weight
    )
    return (first_new, second_new, weight_new)


def mm(a, b, dims):
    return lax.dot_general(a, b, (dims, ((), ())), preferred_element_type=jnp.float32)


def band_start(key_tile, query_tile):
    place = jnp.clip(key_tile - query_tile + BAND // 2, 0, BAND - 1)
    return pl.multiple_of(place * TILE, TILE)


def attend_forward(q_ref, k_ref, v_ref, bias_ref, out_ref, log_ref, scores):
    query_tile = lax.axis_index("ctx") * pl.num_programs(1) + pl.program_id(1)
    tiles = k_ref.shape[0] // TILE
    outs = []
    for head in range(2):
        cols = slice(head * HEAD_DIM, (head + 1) * HEAD_DIM)
        query = q_ref[:, cols] * HEAD_DIM ** (-0.5)
        top = None
        for tile in range(tiles):
            rows = slice(tile * TILE, (tile + 1) * TILE)
            score = mm(k_ref[rows, cols], query, ((1,), (1,)))
            score = score + bias_ref[head, pl.ds(band_start(tile, query_tile), TILE), :]
            scores[head, rows, :] = score
            high = jnp.max(score, axis=0, keepdims=True)
            top = high if top is None else jnp.maximum(top, high)
        total = jnp.zeros_like(top)
        result = jnp.zeros((HEAD_DIM, TILE), jnp.float32)
        for tile in range(tiles):
            rows = slice(tile * TILE, (tile + 1) * TILE)
            weight = jnp.exp(scores[head, rows, :] - top)
            total = total + jnp.sum(weight, axis=0, keepdims=True)
            result = result + mm(v_ref[rows, cols], weight.astype(jnp.bfloat16), ((0,), (0,)))
        outs.append(result / total)
        log_ref[0, pl.ds(head, 1), :] = top + jnp.log(total)
    out_ref[...] = jnp.concatenate(outs, axis=0).T.astype(jnp.bfloat16)


def attend_backward(
    q_ref, g_ref, k_ref, v_ref, bias_ref, log_ref,
    dq_ref, dk_ref, dv_ref, band_ref,
    weights, changes, key_sum, value_sum,
):
    step = pl.program_id(1)
    last = pl.num_programs(1) - 1
    query_tile = lax.axis_index("ctx") * pl.num_programs(1) + step
    tiles = k_ref.shape[0] // TILE

    @pl.when(step == 0)
    def _():
        key_sum[...] = jnp.zeros_like(key_sum)
        value_sum[...] = jnp.zeros_like(value_sum)
        band_ref[...] = jnp.zeros_like(band_ref)

    query_parts = []
    for head in range(2):
        cols = slice(head * HEAD_DIM, (head + 1) * HEAD_DIM)
        query = q_ref[:, cols] * HEAD_DIM ** (-0.5)
        grad = g_ref[:, cols]
        log_total = log_ref[0, pl.ds(head, 1), :]
        row_dot = jnp.zeros_like(log_total)
        for tile in range(tiles):
            rows = slice(tile * TILE, (tile + 1) * TILE)
            start = band_start(tile, query_tile)
            score = mm(k_ref[rows, cols], query, ((1,), (1,)))
            score = score + bias_ref[head, pl.ds(start, TILE), :]
            weight = jnp.exp(score - log_total)
            change = mm(v_ref[rows, cols], grad, ((1,), (1,)))
            row_dot = row_dot + jnp.sum(weight * change, axis=0, keepdims=True)
            weights[head, rows, :] = weight
            changes[head, rows, :] = change
            value_sum[head, rows, :] += mm(weight.astype(jnp.bfloat16), grad, ((1,), (0,)))
        part = jnp.zeros((HEAD_DIM, TILE), jnp.float32)
        for tile in range(tiles):
            rows = slice(tile * TILE, (tile + 1) * TILE)
            start = band_start(tile, query_tile)
            slope = weights[head, rows, :] * (changes[head, rows, :] - row_dot)
            low = slope.astype(jnp.bfloat16)
            band_ref[head, pl.ds(start, TILE), :] += low.astype(jnp.float32)
            part = part + mm(k_ref[rows, cols], low, ((0,), (0,)))
            key_sum[head, rows, :] += mm(low, query, ((1,), (0,)))
        query_parts.append(part)
    query_grad = jnp.concatenate(query_parts, axis=0).T * HEAD_DIM ** (-0.5)
    dq_ref[...] = query_grad.astype(jnp.bfloat16)

    @pl.when(step == last)
    def _():
        dk_ref[...] = jnp.concatenate([key_sum[0], key_sum[1]], axis=1).astype(jnp.bfloat16)
        dv_ref[...] = jnp.concatenate([value_sum[0], value_sum[1]], axis=1).astype(jnp.bfloat16)


def attention_specs(block_len, full_len, pairs):
    query = pl.BlockSpec((TILE, 2 * HEAD_DIM), lambda p, i: (i, p))
    key = pl.BlockSpec((full_len, 2 * HEAD_DIM), lambda p, i: (0, p))
    value = pl.BlockSpec((full_len, 2 * HEAD_DIM), lambda p, i: (0, p + pairs))
    bias = pl.BlockSpec((2, BAND * TILE, TILE), lambda p, i: (p, 0, 0))
    logs = pl.BlockSpec((1, 2, TILE), lambda p, i: (p, 0, i))
    return query, key, value, bias, logs


def run_forward(queries, key_value, bias):
    block_len, width = queries.shape
    full_len = key_value.shape[0]
    pairs = width // (2 * HEAD_DIM)
    query, key, value, strip, logs = attention_specs(block_len, full_len, pairs)
    return pl.pallas_call(
        attend_forward,
        grid=(pairs, block_len // TILE),
        in_specs=[query, key, value, strip],
        out_specs=[query, logs],
        out_shape=[
            jax.ShapeDtypeStruct((block_len, width), jnp.bfloat16),
            jax.ShapeDtypeStruct((pairs, 2, block_len), jnp.float32),
        ],
        scratch_shapes=[pltpu.VMEM((2, full_len, TILE), jnp.float32)],
        compiler_params=pltpu.CompilerParams(vmem_limit_bytes=40 * 2**20),
        cost_estimate=pl.CostEstimate(
            flops=16 * block_len * full_len * width,
            bytes_accessed=20 * 2**20,
            transcendentals=block_len * full_len * width // HEAD_DIM,
        ),
    )(queries, key_value, key_value, bias)


def run_backward(queries, grads, key_value, bias, log_sums):
    block_len, width = queries.shape
    full_len = key_value.shape[0]
    pairs = width // (2 * HEAD_DIM)
    query, key, value, strip, logs = attention_specs(block_len, full_len, pairs)
    whole = jax.ShapeDtypeStruct((full_len, width), jnp.bfloat16)
    return pl.pallas_call(
        attend_backward,
        grid=(pairs, block_len // TILE),
        in_specs=[query, query, key, value, strip, logs],
        out_specs=[query, key, key, strip],
        out_shape=[
            jax.ShapeDtypeStruct((block_len, width), jnp.bfloat16),
            whole,
            whole,
            jax.ShapeDtypeStruct((2 * pairs, BAND * TILE, TILE), jnp.float32),
        ],
        scratch_shapes=[
            pltpu.VMEM((2, full_len, TILE), jnp.float32),
            pltpu.VMEM((2, full_len, TILE), jnp.float32),
            pltpu.VMEM((2, full_len, HEAD_DIM), jnp.float32),
            pltpu.VMEM((2, full_len, HEAD_DIM), jnp.float32),
        ],
        compiler_params=pltpu.CompilerParams(vmem_limit_bytes=48 * 2**20),
        cost_estimate=pl.CostEstimate(
            flops=40 * block_len * full_len * width,
            bytes_accessed=40 * 2**20,
            transcendentals=block_len * full_len * width // HEAD_DIM,
        ),
    )(queries, grads, key_value, key_value, bias, log_sums)


def shards(
    tokens,
    cotangent,
    routes,
    qkv_weight,
    out_weight,
    router_weight,
    bias_table,
    norm_gains,
    expert_in,
    expert_down,
    qkv_first,
    qkv_second,
    out_first,
    out_second,
    router_first,
    router_second,
    table_first,
    table_second,
    gains_first,
    gains_second,
    in_first,
    in_second,
    down_first,
    down_second,
):
    seq_count, block_len, model_width = tokens.shape
    tp_count = lax.axis_size("tp")
    dp_count = lax.axis_size("dp")
    tp_place = lax.axis_index("tp")
    assert seq_count == tp_count and expert_in.shape[0] == 1
    full_len = block_len * lax.axis_size("ctx")
    local_rows, _, local_width = qkv_weight.shape
    expert_count = router_weight.shape[1]
    table_rows, local_heads = bias_table.shape
    bucket_count = table_rows * dp_count
    head_count = local_heads * tp_count
    capacity = max(4, 3 * block_len // (2 * expert_count))
    low = jnp.bfloat16

    small_sizes = (local_rows * expert_count, local_rows * 2, table_rows * local_heads)
    small_count = sum(small_sizes)
    small_rows = -(-small_count // model_width)

    def pack_small(router, gains, table):
        flat = jnp.concatenate([router.reshape(-1), gains.reshape(-1), table.reshape(-1)])
        flat = jnp.pad(flat, (0, small_rows * model_width - small_count))
        return flat.reshape(small_rows, model_width)

    def cut_small(flat):
        ends = (small_sizes[0], small_sizes[0] + small_sizes[1])
        return flat[..., : ends[0]], flat[..., ends[0] : ends[1]], flat[..., ends[1] : small_count]

    main = jnp.concatenate([qkv_weight, out_weight[:, None, :]], axis=1)
    main = jnp.transpose(main, (1, 2, 0)).astype(low).reshape(4 * local_width, local_rows)
    shared = lax.all_gather(main, ("dp", "tp"), axis=0)
    small = lax.all_gather(
        pack_small(router_weight.astype(low), norm_gains.astype(low), bias_table.astype(low)),
        ("dp", "tp"),
        axis=0,
    )
    in_rows = lax.all_gather(expert_in[0].T.astype(low), "tp", axis=0, tiled=True)
    down_rows = lax.all_gather(expert_down[0].astype(low), "tp", axis=0, tiled=True)

    shared = shared.reshape(dp_count, tp_count, 4, local_width, local_rows)
    shared = jnp.transpose(shared, (2, 1, 3, 0, 4)).reshape(4 * model_width, model_width)
    w_qkv = shared[: 3 * model_width]
    w_out = shared[3 * model_width :]
    small = small.reshape(dp_count, tp_count, -1)
    router_flat, gains_flat, table_flat = cut_small(small)
    w_router = router_flat[:, 0].reshape(model_width, expert_count)
    w_gains = gains_flat[:, 0].reshape(model_width, 2)
    w_table = jnp.transpose(
        table_flat.reshape(dp_count, tp_count, table_rows, local_heads), (0, 2, 1, 3)
    ).reshape(bucket_count, head_count)
    gain_one = w_gains[:, 0].astype(jnp.float32)
    gain_two = w_gains[:, 1].astype(jnp.float32)

    strip_keys = jnp.arange(BAND * TILE, dtype=jnp.int32)
    strip_queries = jnp.arange(TILE, dtype=jnp.int32) + (BAND // 2) * TILE
    strip_buckets = bucket_of(strip_queries, strip_keys)
    strip_hot = (
        strip_buckets[None] == jnp.arange(bucket_count, dtype=jnp.int32)[:, None, None]
    ).astype(low)
    bias = jnp.einsum("bh,bkq->hkq", w_table, strip_hot, preferred_element_type=jnp.float32)

    own = lax.dynamic_index_in_dim(tokens, tp_place, 0, keepdims=False)
    inputs = own.astype(jnp.float32)
    normed, norm_one_back = jax.vjp(rms_norm, inputs, gain_one)
    normed_low = normed.astype(low)
    key_value_here = jnp.einsum(
        "rd,cd->rc", normed_low, w_qkv[model_width:], preferred_element_type=jnp.float32
    ).astype(low)
    key_value = lax.all_gather(key_value_here, "ctx", axis=0, tiled=True)
    queries = jnp.einsum(
        "rd,cd->rc", normed_low, w_qkv[:model_width], preferred_element_type=jnp.float32
    ).astype(low)
    mixed_heads, log_sums = run_forward(queries, key_value, bias)
    attention = jnp.einsum("rc,co->ro", mixed_heads, w_out, preferred_element_type=jnp.float32)
    hidden = inputs + attention
    normed_two, norm_two_back = jax.vjp(rms_norm, hidden, gain_two)
    normed_two_low = normed_two.astype(low)
    logits = jnp.dot(normed_two_low, w_router, preferred_element_type=jnp.float32)
    router_probs = jax.nn.softmax(logits, axis=-1)
    route_flat = lax.dynamic_index_in_dim(routes, tp_place, 0, keepdims=False)[:, 0]
    route_hot = (
        route_flat[:, None] == jnp.arange(expert_count, dtype=jnp.int32)[None, :]
    ).astype(jnp.int32)
    earlier = jnp.cumsum(route_hot, axis=0) - route_hot
    slot_index = jnp.sum(earlier * route_hot, axis=-1)
    target = route_flat * capacity + slot_index
    route_mask = route_hot.astype(jnp.float32)
    gate_value = jnp.sum(router_probs * route_mask, axis=-1)
    dispatch_hot = (
        target[None, :] == jnp.arange(expert_count * capacity, dtype=jnp.int32)[:, None]
    ).astype(low)

    def to_experts(rows):
        slots = jnp.dot(dispatch_hot, rows, preferred_element_type=jnp.float32).astype(low)
        return lax.all_to_all(slots, "dp", split_axis=0, concat_axis=0, tiled=True)

    def from_experts(slots):
        back = lax.all_to_all(slots.astype(low), "dp", split_axis=0, concat_axis=0, tiled=True)
        return jnp.einsum("tr,td->rd", dispatch_hot, back, preferred_element_type=jnp.float32)

    upstream = lax.dynamic_index_in_dim(cotangent, tp_place, 0, keepdims=False)
    upstream = upstream.astype(jnp.float32)
    row_grad = (gate_value[:, None] * upstream).astype(low)
    arrived = to_experts(normed_two_low)
    grad_arrived = to_experts(row_grad)
    pre_act = jnp.einsum("md,fd->mf", arrived, in_rows, preferred_element_type=jnp.float32)
    activated, gelu_back = jax.vjp(lambda a: jax.nn.gelu(a, approximate=True), pre_act)
    active_low = activated.astype(low)
    down_slots = jnp.dot(active_low, down_rows, preferred_element_type=jnp.float32)
    expert_rows = from_experts(down_slots)
    act_grad = jnp.einsum("md,fd->mf", grad_arrived, down_rows, preferred_element_type=jnp.float32)
    pre_grad = gelu_back(act_grad)[0].astype(low)
    slot_back = jnp.dot(pre_grad, in_rows, preferred_element_type=jnp.float32)
    expert_backward_rows = from_experts(slot_back)
    grad_down = jnp.einsum(
        "mf,md->fd", active_low, grad_arrived, preferred_element_type=jnp.float32
    ).astype(low)
    grad_in = jnp.einsum(
        "mf,md->fd", pre_grad, arrived, preferred_element_type=jnp.float32
    ).astype(low)
    grad_down = lax.psum_scatter(grad_down, "tp", scatter_dimension=0, tiled=True)
    grad_in = lax.psum_scatter(grad_in, "tp", scatter_dimension=0, tiled=True)
    grad_down, grad_in = lax.psum((grad_down, grad_in), "ctx")

    mixed_here = (hidden + gate_value[:, None] * expert_rows).astype(low)
    mixed_out = lax.all_gather(mixed_here, "tp", axis=0)
    gate_grad = jnp.sum(upstream * expert_rows, axis=-1)
    prob_grad = route_mask * gate_grad[:, None]
    logit_grad = (
        router_probs * (prob_grad - jnp.sum(prob_grad * router_probs, axis=-1, keepdims=True))
    ).astype(low)
    grad_router = jnp.einsum(
        "rd,re->de", normed_two_low, logit_grad, preferred_element_type=jnp.float32
    )
    normed_two_grad = expert_backward_rows + jnp.einsum(
        "re,de->rd", logit_grad, w_router, preferred_element_type=jnp.float32
    )
    hidden_back, gain_two_grad = norm_two_back(normed_two_grad)
    hidden_grad = upstream + hidden_back
    hidden_low = hidden_grad.astype(low)
    grad_out = jnp.einsum("rc,ro->co", mixed_heads, hidden_low, preferred_element_type=jnp.float32)
    heads_grad = jnp.einsum(
        "ro,co->rc", hidden_low, w_out, preferred_element_type=jnp.float32
    ).astype(low)
    query_grad, key_grad, value_grad, strip_grad = run_backward(
        queries, heads_grad, key_value, bias, log_sums
    )
    key_grad = lax.psum_scatter(key_grad, "ctx", scatter_dimension=0, tiled=True)
    value_grad = lax.psum_scatter(value_grad, "ctx", scatter_dimension=0, tiled=True)
    grad_table = jnp.einsum(
        "hkq,bkq->bh", strip_grad, strip_hot, preferred_element_type=jnp.float32
    )
    projected_grad = jnp.concatenate([query_grad, key_grad, value_grad], axis=1)
    grad_qkv = jnp.einsum(
        "rc,rd->cd", projected_grad, normed_low, preferred_element_type=jnp.float32
    )
    normed_grad = jnp.einsum(
        "rc,cd->rd", projected_grad, w_qkv, preferred_element_type=jnp.float32
    )
    input_back, gain_one_grad = norm_one_back(normed_grad)
    tokens_grad = lax.all_gather((hidden_grad + input_back).astype(low), "tp", axis=0)
    tokens_grad = tokens_grad.astype(jnp.float32)
    grad_gains = jnp.stack([gain_one_grad, gain_two_grad], axis=1)

    main_grad = jnp.concatenate([grad_qkv, grad_out], axis=0).astype(low)
    main_grad = main_grad.reshape(4, tp_count, local_width, dp_count, local_rows)
    main_grad = jnp.transpose(main_grad, (3, 1, 0, 2, 4)).reshape(-1, local_rows)
    main_grad = lax.psum_scatter(main_grad, ("dp", "tp"), scatter_dimension=0, tiled=True)
    main_grad = lax.psum(main_grad, "ctx").reshape(4, local_width, local_rows)
    main_grad = jnp.transpose(main_grad, (2, 0, 1)).astype(jnp.float32)
    small_grad = lax.psum(
        jnp.concatenate([grad_router.reshape(-1), grad_gains.reshape(-1), grad_table.reshape(-1)]),
        ("dp", "ctx", "tp"),
    )
    dp_place = lax.axis_index("dp")
    ends = (model_width * expert_count, model_width * (expert_count + 2))
    router_total = small_grad[: ends[0]].reshape(model_width, expert_count)
    gains_total = small_grad[ends[0] : ends[1]].reshape(model_width, 2)
    table_total = small_grad[ends[1] :].reshape(bucket_count, head_count)
    router_total = lax.dynamic_slice_in_dim(router_total, dp_place * local_rows, local_rows, 0)
    gains_total = lax.dynamic_slice_in_dim(gains_total, dp_place * local_rows, local_rows, 0)
    table_total = lax.dynamic_slice(
        table_total,
        (dp_place * table_rows, tp_place * local_heads),
        (table_rows, local_heads),
    )

    qkv_new = adamw(qkv_weight, main_grad[:, :3], qkv_first, qkv_second, 2.0 * D ** (-0.5))
    out_new = adamw(
        out_weight, main_grad[:, 3], out_first, out_second, 2.0 * max(1, 8 * D // LENGTH) ** (-0.5)
    )
    router_new = adamw(
        router_weight, router_total, router_first, router_second, 2.0 * (2 * D) ** (-0.5)
    )
    table_new = adamw(bias_table, table_total, table_first, table_second, 2.0)
    gains_new = adamw(norm_gains, gains_total, gains_first, gains_second, 0.25)
    in_new = adamw(
        expert_in,
        grad_in.T[None].astype(jnp.float32),
        in_first,
        in_second,
        2.0 * D ** (-0.5),
    )
    down_new = adamw(
        expert_down,
        grad_down[None].astype(jnp.float32),
        down_first,
        down_second,
        2.0 * max(1, FF // (expert_count * expert_count)) ** (-0.5),
    )
    return (
        mixed_out,
        tokens_grad,
        *qkv_new,
        *out_new,
        *router_new,
        *table_new,
        *gains_new,
        *in_new,
        *down_new,
    )


def solution(mesh):
    in_specs = (
        P("dp", "ctx", None),
        P("dp", "ctx", None),
        P("dp", "ctx", None),
        P("dp", None, "tp"),
        P("dp", "tp"),
        P("dp", None),
        P("dp", "tp"),
        P("dp", None),
        P("dp", None, "tp"),
        P("dp", "tp", None),
        P("dp", None, "tp"),
        P("dp", None, "tp"),
        P("dp", "tp"),
        P("dp", "tp"),
        P("dp", None),
        P("dp", None),
        P("dp", "tp"),
        P("dp", "tp"),
        P("dp", None),
        P("dp", None),
        P("dp", None, "tp"),
        P("dp", None, "tp"),
        P("dp", "tp", None),
        P("dp", "tp", None),
    )
    out_specs = (
        P("dp", "ctx", None),
        P("dp", "ctx", None),
        P("dp", None, "tp"),
        P("dp", None, "tp"),
        P("dp", None, "tp"),
        P("dp", "tp"),
        P("dp", "tp"),
        P("dp", "tp"),
        P("dp", None),
        P("dp", None),
        P("dp", None),
        P("dp", "tp"),
        P("dp", "tp"),
        P("dp", "tp"),
        P("dp", None),
        P("dp", None),
        P("dp", None),
        P("dp", None, "tp"),
        P("dp", None, "tp"),
        P("dp", None, "tp"),
        P("dp", "tp", None),
        P("dp", "tp", None),
        P("dp", "tp", None),
    )
    return jax.shard_map(shards, mesh=mesh, in_specs=in_specs, out_specs=out_specs, check_vma=False)
```

```python
import jax
import jax.numpy as jnp
from jax import lax
from jax.experimental import pallas as pl
from jax.experimental.pallas import tpu as pltpu
from jax.sharding import PartitionSpec as P

D = 768
HEAD_DIM = 64
FF = 3072
LENGTH = 2048
STEP = 10
TILE = 256
BAND = 5


thresholds = (12, 16, 23, 32, 46, 64, 91)
beta_one = 0.9
beta_two = 0.999
epsilon = 1e-08
decay = 0.01


def bucket_of(query_pos, key_pos):
    offset = key_pos[:, None] - query_pos[None, :]
    distance = jnp.abs(offset)
    bucket = jnp.minimum(distance, 8)
    for border in thresholds:
        bucket = bucket + (distance >= border).astype(jnp.int32)
    return bucket + 16 * (offset > 0).astype(jnp.int32)


def rms_norm(values, gain_vector_row):
    return (
        values
        * lax.rsqrt(jnp.mean(values * values, axis=-1, keepdims=True) + 1e-06)
        * gain_vector_row
    )


def adamw(weight, gradient, moment_one, moment_two, step_rate):
    first_new = beta_one * moment_one + (1.0 - beta_one) * gradient
    second_new = beta_two * moment_two + (1.0 - beta_two) * gradient * gradient
    corrected_first = first_new / (1.0 - beta_one**STEP)
    corrected_second = second_new / (1.0 - beta_two**STEP)
    weight_new = weight - step_rate * (
        corrected_first / (jnp.sqrt(corrected_second) + epsilon) + decay * weight
    )
    return (first_new, second_new, weight_new)


def mm(a, b, dims):
    return lax.dot_general(a, b, (dims, ((), ())), preferred_element_type=jnp.float32)


def band_start(key_tile, query_tile):
    place = jnp.clip(key_tile - query_tile + BAND // 2, 0, BAND - 1)
    return pl.multiple_of(place * TILE, TILE)


def attend_forward(q_ref, k_ref, v_ref, bias_ref, out_ref, log_ref, scores):
    query_tile = lax.axis_index("ctx") * pl.num_programs(1) + pl.program_id(1)
    tiles = k_ref.shape[0] // TILE
    outs = []
    for head in range(2):
        cols = slice(head * HEAD_DIM, (head + 1) * HEAD_DIM)
        query = q_ref[:, cols] * HEAD_DIM ** (-0.5)
        top = None
        for tile in range(tiles):
            rows = slice(tile * TILE, (tile + 1) * TILE)
            score = mm(k_ref[rows, cols], query, ((1,), (1,)))
            score = score + bias_ref[head, pl.ds(band_start(tile, query_tile), TILE), :]
            scores[head, rows, :] = score
            high = jnp.max(score, axis=0, keepdims=True)
            top = high if top is None else jnp.maximum(top, high)
        total = jnp.zeros_like(top)
        result = jnp.zeros((HEAD_DIM, TILE), jnp.float32)
        for tile in range(tiles):
            rows = slice(tile * TILE, (tile + 1) * TILE)
            weight = jnp.exp(scores[head, rows, :] - top)
            total = total + jnp.sum(weight, axis=0, keepdims=True)
            result = result + mm(v_ref[rows, cols], weight.astype(jnp.bfloat16), ((0,), (0,)))
        outs.append(result / total)
        log_ref[0, pl.ds(head, 1), :] = top + jnp.log(total)
    out_ref[...] = jnp.concatenate(outs, axis=0).T.astype(jnp.bfloat16)


def attend_backward(
    q_ref, g_ref, k_ref, v_ref, bias_ref, log_ref,
    dq_ref, dk_ref, dv_ref, band_ref,
    weights, changes, key_sum, value_sum,
):
    step = pl.program_id(1)
    last = pl.num_programs(1) - 1
    query_tile = lax.axis_index("ctx") * pl.num_programs(1) + step
    tiles = k_ref.shape[0] // TILE

    @pl.when(step == 0)
    def _():
        key_sum[...] = jnp.zeros_like(key_sum)
        value_sum[...] = jnp.zeros_like(value_sum)
        band_ref[...] = jnp.zeros_like(band_ref)

    query_parts = []
    for head in range(2):
        cols = slice(head * HEAD_DIM, (head + 1) * HEAD_DIM)
        query = q_ref[:, cols] * HEAD_DIM ** (-0.5)
        grad = g_ref[:, cols]
        log_total = log_ref[0, pl.ds(head, 1), :]
        row_dot = jnp.zeros_like(log_total)
        for tile in range(tiles):
            rows = slice(tile * TILE, (tile + 1) * TILE)
            start = band_start(tile, query_tile)
            score = mm(k_ref[rows, cols], query, ((1,), (1,)))
            score = score + bias_ref[head, pl.ds(start, TILE), :]
            weight = jnp.exp(score - log_total)
            change = mm(v_ref[rows, cols], grad, ((1,), (1,)))
            row_dot = row_dot + jnp.sum(weight * change, axis=0, keepdims=True)
            weights[head, rows, :] = weight
            changes[head, rows, :] = change
            value_sum[head, rows, :] += mm(weight.astype(jnp.bfloat16), grad, ((1,), (0,)))
        part = jnp.zeros((HEAD_DIM, TILE), jnp.float32)
        for tile in range(tiles):
            rows = slice(tile * TILE, (tile + 1) * TILE)
            start = band_start(tile, query_tile)
            slope = weights[head, rows, :] * (changes[head, rows, :] - row_dot)
            low = slope.astype(jnp.bfloat16)
            band_ref[head, pl.ds(start, TILE), :] += low.astype(jnp.float32)
            part = part + mm(k_ref[rows, cols], low, ((0,), (0,)))
            key_sum[head, rows, :] += mm(low, query, ((1,), (0,)))
        query_parts.append(part)
    query_grad = jnp.concatenate(query_parts, axis=0).T * HEAD_DIM ** (-0.5)
    dq_ref[...] = query_grad.astype(jnp.bfloat16)

    @pl.when(step == last)
    def _():
        dk_ref[...] = jnp.concatenate([key_sum[0], key_sum[1]], axis=1).astype(jnp.bfloat16)
        dv_ref[...] = jnp.concatenate([value_sum[0], value_sum[1]], axis=1).astype(jnp.bfloat16)


def attention_specs(block_len, full_len, pairs):
    query = pl.BlockSpec((TILE, 2 * HEAD_DIM), lambda p, i: (i, p))
    key = pl.BlockSpec((full_len, 2 * HEAD_DIM), lambda p, i: (0, p))
    value = pl.BlockSpec((full_len, 2 * HEAD_DIM), lambda p, i: (0, p + pairs))
    bias = pl.BlockSpec((2, BAND * TILE, TILE), lambda p, i: (p, 0, 0))
    logs = pl.BlockSpec((1, 2, TILE), lambda p, i: (p, 0, i))
    return query, key, value, bias, logs


def run_forward(queries, key_value, bias):
    block_len, width = queries.shape
    full_len = key_value.shape[0]
    pairs = width // (2 * HEAD_DIM)
    query, key, value, strip, logs = attention_specs(block_len, full_len, pairs)
    return pl.pallas_call(
        attend_forward,
        grid=(pairs, block_len // TILE),
        in_specs=[query, key, value, strip],
        out_specs=[query, logs],
        out_shape=[
            jax.ShapeDtypeStruct((block_len, width), jnp.bfloat16),
            jax.ShapeDtypeStruct((pairs, 2, block_len), jnp.float32),
        ],
        scratch_shapes=[pltpu.VMEM((2, full_len, TILE), jnp.float32)],
        compiler_params=pltpu.CompilerParams(vmem_limit_bytes=40 * 2**20),
        cost_estimate=pl.CostEstimate(
            flops=16 * block_len * full_len * width,
            bytes_accessed=20 * 2**20,
            transcendentals=block_len * full_len * width // HEAD_DIM,
        ),
    )(queries, key_value, key_value, bias)


def run_backward(queries, grads, key_value, bias, log_sums):
    block_len, width = queries.shape
    full_len = key_value.shape[0]
    pairs = width // (2 * HEAD_DIM)
    query, key, value, strip, logs = attention_specs(block_len, full_len, pairs)
    whole = jax.ShapeDtypeStruct((full_len, width), jnp.bfloat16)
    return pl.pallas_call(
        attend_backward,
        grid=(pairs, block_len // TILE),
        in_specs=[query, query, key, value, strip, logs],
        out_specs=[query, key, key, strip],
        out_shape=[
            jax.ShapeDtypeStruct((block_len, width), jnp.bfloat16),
            whole,
            whole,
            jax.ShapeDtypeStruct((2 * pairs, BAND * TILE, TILE), jnp.float32),
        ],
        scratch_shapes=[
            pltpu.VMEM((2, full_len, TILE), jnp.float32),
            pltpu.VMEM((2, full_len, TILE), jnp.float32),
            pltpu.VMEM((2, full_len, HEAD_DIM), jnp.float32),
            pltpu.VMEM((2, full_len, HEAD_DIM), jnp.float32),
        ],
        compiler_params=pltpu.CompilerParams(vmem_limit_bytes=48 * 2**20),
        cost_estimate=pl.CostEstimate(
            flops=40 * block_len * full_len * width,
            bytes_accessed=40 * 2**20,
            transcendentals=block_len * full_len * width // HEAD_DIM,
        ),
    )(queries, grads, key_value, key_value, bias, log_sums)


def shards(
    tokens,
    cotangent,
    routes,
    qkv_weight,
    out_weight,
    router_weight,
    bias_table,
    norm_gains,
    expert_in,
    expert_down,
    qkv_first,
    qkv_second,
    out_first,
    out_second,
    router_first,
    router_second,
    table_first,
    table_second,
    gains_first,
    gains_second,
    in_first,
    in_second,
    down_first,
    down_second,
):
    seq_count, block_len, model_width = tokens.shape
    tp_count = lax.axis_size("tp")
    dp_count = lax.axis_size("dp")
    tp_place = lax.axis_index("tp")
    assert seq_count == tp_count and expert_in.shape[0] == 1
    full_len = block_len * lax.axis_size("ctx")
    local_rows, _, local_width = qkv_weight.shape
    expert_count = router_weight.shape[1]
    table_rows, local_heads = bias_table.shape
    bucket_count = table_rows * dp_count
    head_count = local_heads * tp_count
    capacity = max(4, 3 * block_len // (2 * expert_count))
    low = jnp.bfloat16

    ctx_count = lax.axis_size("ctx")
    pairs = [[i, i + 1] for i in range(0, ctx_count, 2)]
    side = lax.rem(lax.axis_index("ctx"), 2)
    small_sizes = (local_rows * expert_count, local_rows * 2, table_rows * local_heads)
    small_count = sum(small_sizes)
    main_rows = 4 * local_width
    pack_rows = -(-(main_rows + -(-small_count // local_rows)) // 32) * 32
    small_room = (pack_rows - main_rows) * local_rows

    def half(rows):
        count = rows.shape[0] // 2
        return lax.dynamic_slice_in_dim(rows, side * count, count, 0)

    def pair_gather(rows, axis):
        return lax.all_gather(rows, "ctx", axis=axis, axis_index_groups=pairs, tiled=True)

    def pair_scatter(rows):
        return lax.psum_scatter(
            rows, "ctx", scatter_dimension=0, axis_index_groups=pairs, tiled=True
        )

    def ctx_sum(rows):
        every = lax.all_gather(rows, "ctx", axis=0).astype(jnp.float32)
        total = jnp.sum(every.reshape((ctx_count // 2, 2) + rows.shape), axis=0)
        return total.reshape((2 * rows.shape[0],) + rows.shape[1:])

    def pack_small(router, gains, table):
        lead = router.shape[:-2]
        flat = jnp.concatenate([a.reshape(lead + (-1,)) for a in (router, gains, table)], axis=-1)
        flat = jnp.pad(flat, [(0, 0)] * len(lead) + [(0, small_room - small_count)])
        return flat.reshape(lead + (pack_rows - main_rows, local_rows))

    def cut_small(flat):
        ends = (small_sizes[0], small_sizes[0] + small_sizes[1])
        return flat[..., : ends[0]], flat[..., ends[0] : ends[1]], flat[..., ends[1] : small_count]

    main = jnp.concatenate([qkv_weight, out_weight[:, None, :]], axis=1)
    main = jnp.transpose(main, (1, 2, 0)).astype(low).reshape(main_rows, local_rows)
    small = pack_small(router_weight.astype(low), norm_gains.astype(low), bias_table.astype(low))
    packed = half(jnp.concatenate([main, small], axis=0))
    packed = pair_gather(lax.all_gather(packed, ("dp", "tp"), axis=0), 1)
    in_half = lax.all_gather(half(expert_in[0].T.astype(low)), "tp", axis=0, tiled=True)
    in_rows = pair_gather(in_half, 0)
    down_half = lax.all_gather(half(expert_down[0].astype(low)), "tp", axis=0, tiled=True)
    down_rows = pair_gather(down_half, 0)

    shared = packed[:, :main_rows].reshape(dp_count, tp_count, 4, local_width, local_rows)
    shared = jnp.transpose(shared, (2, 1, 3, 0, 4)).reshape(4 * model_width, model_width)
    w_qkv = shared[: 3 * model_width]
    w_out = shared[3 * model_width :]
    small = packed[:, main_rows:].reshape(dp_count, tp_count, -1)
    router_flat, gains_flat, table_flat = cut_small(small)
    w_router = router_flat[:, 0].reshape(model_width, expert_count)
    w_gains = gains_flat[:, 0].reshape(model_width, 2)
    w_table = jnp.transpose(
        table_flat.reshape(dp_count, tp_count, table_rows, local_heads), (0, 2, 1, 3)
    ).reshape(bucket_count, head_count)
    gain_one = w_gains[:, 0].astype(jnp.float32)
    gain_two = w_gains[:, 1].astype(jnp.float32)

    strip_keys = jnp.arange(BAND * TILE, dtype=jnp.int32)
    strip_queries = jnp.arange(TILE, dtype=jnp.int32) + (BAND // 2) * TILE
    strip_buckets = bucket_of(strip_queries, strip_keys)
    strip_hot = (
        strip_buckets[None] == jnp.arange(bucket_count, dtype=jnp.int32)[:, None, None]
    ).astype(low)
    bias = jnp.einsum("bh,bkq->hkq", w_table, strip_hot, preferred_element_type=jnp.float32)

    own = lax.dynamic_index_in_dim(tokens, tp_place, 0, keepdims=False)
    inputs = own.astype(jnp.float32)
    normed, norm_one_back = jax.vjp(rms_norm, inputs, gain_one)
    normed_low = normed.astype(low)
    key_value_here = jnp.einsum(
        "rd,cd->rc", normed_low, w_qkv[model_width:], preferred_element_type=jnp.float32
    ).astype(low)
    key_value = lax.all_gather(key_value_here, "ctx", axis=0, tiled=True)
    queries = jnp.einsum(
        "rd,cd->rc", normed_low, w_qkv[:model_width], preferred_element_type=jnp.float32
    ).astype(low)
    mixed_heads, log_sums = run_forward(queries, key_value, bias)
    attention = jnp.einsum("rc,co->ro", mixed_heads, w_out, preferred_element_type=jnp.float32)
    hidden = inputs + attention
    normed_two, norm_two_back = jax.vjp(rms_norm, hidden, gain_two)
    normed_two_low = normed_two.astype(low)
    logits = jnp.dot(normed_two_low, w_router, preferred_element_type=jnp.float32)
    router_probs = jax.nn.softmax(logits, axis=-1)
    route_flat = lax.dynamic_index_in_dim(routes, tp_place, 0, keepdims=False)[:, 0]
    route_hot = (
        route_flat[:, None] == jnp.arange(expert_count, dtype=jnp.int32)[None, :]
    ).astype(jnp.int32)
    earlier = jnp.cumsum(route_hot, axis=0) - route_hot
    slot_index = jnp.sum(earlier * route_hot, axis=-1)
    target = route_flat * capacity + slot_index
    route_mask = route_hot.astype(jnp.float32)
    gate_value = jnp.sum(router_probs * route_mask, axis=-1)
    dispatch_hot = (
        target[None, :] == jnp.arange(expert_count * capacity, dtype=jnp.int32)[:, None]
    ).astype(low)

    dp_place = lax.axis_index("dp")

    def to_experts(rows):
        slots = jnp.dot(dispatch_hot, rows, preferred_element_type=jnp.float32).astype(low)
        if dp_count != 2:
            return [lax.all_to_all(slots, "dp", split_axis=0, concat_axis=0, tiled=True)]
        sent = lax.dynamic_slice_in_dim(slots, (1 - dp_place) * capacity, capacity, 0)
        kept = lax.dynamic_slice_in_dim(slots, dp_place * capacity, capacity, 0)
        return [kept, lax.ppermute(sent, "dp", [(0, 1), (1, 0)])]

    def from_experts(parts):
        parts = [part.astype(low) for part in parts]
        if dp_count != 2:
            back = lax.all_to_all(parts[0], "dp", split_axis=0, concat_axis=0, tiled=True)
            return jnp.einsum("tr,td->rd", dispatch_hot, back, preferred_element_type=jnp.float32)
        other = lax.ppermute(parts[1], "dp", [(0, 1), (1, 0)])
        first = jnp.where(dp_place == 0, parts[0], other)
        second = jnp.where(dp_place == 0, other, parts[0])
        back = jnp.concatenate([first, second], axis=0)
        return jnp.einsum("tr,td->rd", dispatch_hot, back, preferred_element_type=jnp.float32)

    upstream = lax.dynamic_index_in_dim(cotangent, tp_place, 0, keepdims=False)
    upstream = upstream.astype(jnp.float32)
    row_grad = (gate_value[:, None] * upstream).astype(low)
    arrived = to_experts(normed_two_low)
    grad_arrived = to_experts(row_grad)
    actives, downs, pre_grads, backs = [], [], [], []
    for rows, grads in zip(arrived, grad_arrived):
        pre_act = jnp.einsum("md,fd->mf", rows, in_rows, preferred_element_type=jnp.float32)
        activated, gelu_back = jax.vjp(lambda a: jax.nn.gelu(a, approximate=True), pre_act)
        active_low = activated.astype(low)
        downs.append(jnp.dot(active_low, down_rows, preferred_element_type=jnp.float32))
        act_grad = jnp.einsum("md,fd->mf", grads, down_rows, preferred_element_type=jnp.float32)
        pre_grad = gelu_back(act_grad)[0].astype(low)
        backs.append(jnp.dot(pre_grad, in_rows, preferred_element_type=jnp.float32))
        actives.append(active_low)
        pre_grads.append(pre_grad)
    expert_rows = from_experts(downs)
    expert_backward_rows = from_experts(backs)
    grad_down = jnp.einsum(
        "mf,md->fd",
        jnp.concatenate(actives, axis=0),
        jnp.concatenate(grad_arrived, axis=0),
        preferred_element_type=jnp.float32,
    ).astype(low)
    grad_in = jnp.einsum(
        "mf,md->fd",
        jnp.concatenate(pre_grads, axis=0),
        jnp.concatenate(arrived, axis=0),
        preferred_element_type=jnp.float32,
    ).astype(low)

    mixed_here = (hidden + gate_value[:, None] * expert_rows).astype(low)
    mixed_out = lax.all_gather(mixed_here, "tp", axis=0)
    gate_grad = jnp.sum(upstream * expert_rows, axis=-1)
    prob_grad = route_mask * gate_grad[:, None]
    logit_grad = (
        router_probs * (prob_grad - jnp.sum(prob_grad * router_probs, axis=-1, keepdims=True))
    ).astype(low)
    grad_router = jnp.einsum(
        "rd,re->de", normed_two_low, logit_grad, preferred_element_type=jnp.float32
    )
    normed_two_grad = expert_backward_rows + jnp.einsum(
        "re,de->rd", logit_grad, w_router, preferred_element_type=jnp.float32
    )
    hidden_back, gain_two_grad = norm_two_back(normed_two_grad)
    hidden_grad = upstream + hidden_back
    hidden_low = hidden_grad.astype(low)
    grad_out = jnp.einsum("rc,ro->co", mixed_heads, hidden_low, preferred_element_type=jnp.float32)
    heads_grad = jnp.einsum(
        "ro,co->rc", hidden_low, w_out, preferred_element_type=jnp.float32
    ).astype(low)
    heads_grad, grad_down, grad_in = lax.optimization_barrier((heads_grad, grad_down, grad_in))
    grad_down = lax.psum_scatter(pair_scatter(grad_down), "tp", scatter_dimension=0, tiled=True)
    grad_in = lax.psum_scatter(pair_scatter(grad_in), "tp", scatter_dimension=0, tiled=True)
    grad_down, grad_in = ctx_sum(grad_down), ctx_sum(grad_in)
    query_grad, key_grad, value_grad, strip_grad = run_backward(
        queries, heads_grad, key_value, bias, log_sums
    )
    key_grad = lax.psum_scatter(key_grad, "ctx", scatter_dimension=0, tiled=True)
    value_grad = lax.psum_scatter(value_grad, "ctx", scatter_dimension=0, tiled=True)
    grad_table = jnp.einsum(
        "hkq,bkq->bh", strip_grad, strip_hot, preferred_element_type=jnp.float32
    )
    projected_grad = jnp.concatenate([query_grad, key_grad, value_grad], axis=1)
    grad_qkv = jnp.einsum(
        "rc,rd->cd", projected_grad, normed_low, preferred_element_type=jnp.float32
    )
    normed_grad = jnp.einsum(
        "rc,cd->rd", projected_grad, w_qkv, preferred_element_type=jnp.float32
    )
    input_back, gain_one_grad = norm_one_back(normed_grad)
    tokens_grad = lax.all_gather((hidden_grad + input_back).astype(low), "tp", axis=0)
    tokens_grad = tokens_grad.astype(jnp.float32)
    grad_gains = jnp.stack([gain_one_grad, gain_two_grad], axis=1)

    main_grad = jnp.concatenate([grad_qkv, grad_out], axis=0).astype(low)
    main_grad = main_grad.reshape(4, tp_count, local_width, dp_count, local_rows)
    main_grad = jnp.transpose(main_grad, (3, 1, 0, 2, 4)).reshape(
        dp_count, tp_count, main_rows, local_rows
    )
    owners = (dp_count, tp_count)

    def by_rows(grad):
        split = grad.reshape(dp_count, 1, local_rows, -1)
        return jnp.broadcast_to(split, owners + split.shape[2:])

    table_split = grad_table.reshape(dp_count, table_rows, tp_count, local_heads)
    small_grad = pack_small(
        by_rows(grad_router), by_rows(grad_gains), jnp.transpose(table_split, (0, 2, 1, 3))
    ).astype(low)
    packed_grad = jnp.concatenate([main_grad, small_grad], axis=2)
    packed_grad = packed_grad.reshape(dp_count * tp_count, 2, pack_rows // 2, local_rows)
    packed_grad = jnp.transpose(packed_grad, (1, 0, 2, 3)).reshape(-1, local_rows)
    packed_grad = lax.psum_scatter(
        pair_scatter(packed_grad), ("dp", "tp"), scatter_dimension=0, tiled=True
    )
    packed_grad = ctx_sum(packed_grad)
    main_grad = packed_grad[:main_rows].reshape(4, local_width, local_rows)
    main_grad = jnp.transpose(main_grad, (2, 0, 1))
    router_total, gains_total, table_total = cut_small(packed_grad[main_rows:].reshape(-1))
    router_total = router_total.reshape(local_rows, expert_count)
    gains_total = gains_total.reshape(local_rows, 2)
    table_total = table_total.reshape(table_rows, local_heads)

    qkv_new = adamw(qkv_weight, main_grad[:, :3], qkv_first, qkv_second, 2.0 * D ** (-0.5))
    out_new = adamw(
        out_weight, main_grad[:, 3], out_first, out_second, 2.0 * max(1, 8 * D // LENGTH) ** (-0.5)
    )
    router_new = adamw(
        router_weight, router_total, router_first, router_second, 2.0 * (2 * D) ** (-0.5)
    )
    table_new = adamw(bias_table, table_total, table_first, table_second, 2.0)
    gains_new = adamw(norm_gains, gains_total, gains_first, gains_second, 0.25)
    in_new = adamw(
        expert_in,
        grad_in.T[None],
        in_first,
        in_second,
        2.0 * D ** (-0.5),
    )
    down_new = adamw(
        expert_down,
        grad_down[None],
        down_first,
        down_second,
        2.0 * max(1, FF // (expert_count * expert_count)) ** (-0.5),
    )
    return (
        mixed_out,
        tokens_grad,
        *qkv_new,
        *out_new,
        *router_new,
        *table_new,
        *gains_new,
        *in_new,
        *down_new,
    )


def solution(mesh):
    in_specs = (
        P("dp", "ctx", None),
        P("dp", "ctx", None),
        P("dp", "ctx", None),
        P("dp", None, "tp"),
        P("dp", "tp"),
        P("dp", None),
        P("dp", "tp"),
        P("dp", None),
        P("dp", None, "tp"),
        P("dp", "tp", None),
        P("dp", None, "tp"),
        P("dp", None, "tp"),
        P("dp", "tp"),
        P("dp", "tp"),
        P("dp", None),
        P("dp", None),
        P("dp", "tp"),
        P("dp", "tp"),
        P("dp", None),
        P("dp", None),
        P("dp", None, "tp"),
        P("dp", None, "tp"),
        P("dp", "tp", None),
        P("dp", "tp", None),
    )
    out_specs = (
        P("dp", "ctx", None),
        P("dp", "ctx", None),
        P("dp", None, "tp"),
        P("dp", None, "tp"),
        P("dp", None, "tp"),
        P("dp", "tp"),
        P("dp", "tp"),
        P("dp", "tp"),
        P("dp", None),
        P("dp", None),
        P("dp", None),
        P("dp", "tp"),
        P("dp", "tp"),
        P("dp", "tp"),
        P("dp", None),
        P("dp", None),
        P("dp", None),
        P("dp", None, "tp"),
        P("dp", None, "tp"),
        P("dp", None, "tp"),
        P("dp", "tp", None),
        P("dp", "tp", None),
        P("dp", "tp", None),
    )
    return jax.shard_map(shards, mesh=mesh, in_specs=in_specs, out_specs=out_specs, check_vma=False)
```
